32 devices in a mesh: row: 4 (over z), col: 4 (over y, x), freq: 2 (over core).
Axes of the slice: x: 2, y: 2, z: 4, core: 2. Of those that a mesh axis runs over, the one named last changes fastest.
Arguments:
- spectra: bfloat16 [10240, 4096], P(('row', 'col'), 'freq'), parts along dimension 1, may hold values from -6 to 6
- loading: float32 [20480], P('freq'), parts along dimension 0, may hold values from 0.05 to 0.5
- delays: int32 [10240, 512], P('row', 'col'), may hold values from 0 to 1023
- bin_index: int32 [2], P('freq'), parts along dimension 0, may hold values from 1 to 1023
Outputs:
- trailing: float32 [20480, 10240], P(('freq', 'row'), 'col'), parts along dimension 0
- panel: float32 [20480, 512], P(('freq', 'row')), parts along dimension 0
- whitened: float32 [2, 20480, 512], P(None, ('freq', 'row'), 'col'), parts along dimension 1
The draws below stay inside these ranges and needn't reach their ends.
There are 2 independent parts, one for each index of `freq`. The reference program is written for one: setup_inputs(seed, part) draws one part's arguments, and reference() takes and returns one part's arrays. A program takes and returns all parts, laid end to end along the dimension named above; an argument that names none is the same for every part. Nothing has to cross between parts.
All inputs are finite; a program needn't handle non-finite values.
Results may differ from the reference program's by a relative error of at most 0.0003.
Values may be sent and summed in bfloat16 or wider, within the bound.
No kernel may reach another device: no remote copies, remote signals or barrier semaphores. Data moves between devices by JAX's collectives and lax.ppermute only.
A program may use at most 192 MiB of HBM per device.

```python
import math
import jax
import jax.numpy as jnp
from jax import lax

C = 10240
SNAP = 1024
PANEL = 512
NFFT = 2048
MAXDELAY = 1024
NSLOW = 512


def place_ends(drawn, own_key, low, top_value):
    longest = drawn.shape.index(max(drawn.shape))
    spots = []
    for shift in (0, 1):
        where = [jax.random.randint(jax.random.fold_in(own_key, axis), (), 0, length) for axis, length in enumerate(drawn.shape)]
        where[longest] = (where[longest] + shift) % drawn.shape[longest]
        spots.append(tuple(where))
    return drawn.at[spots[0]].set(low).at[spots[1]].set(top_value)


def steps_of(rng, extent, shards, least, largest):
    def one(dim, shards_of):
        draws = jax.random.uniform(jax.random.fold_in(jax.random.fold_in(rng, 6), dim), (shards_of,), jnp.float32, least / len(shards), largest / len(shards))
        return jnp.repeat(jnp.exp(draws), extent[dim] // shards_of).reshape((-1,) + (1,) * (len(extent) - dim - 1))

    level = one(*shards[0])
    for cut in shards[1:]:
        level = level * one(*cut)
    return level


def scatter_about(own_key, shape, spread, limit, split=(), dtype=jnp.bfloat16):
    level = steps_of(own_key, shape, split, -0.22, 0.18) if split else 1.0
    array = jax.random.normal(own_key, shape, jnp.float32) * spread * level
    return jnp.minimum(jnp.maximum(array, -limit), limit).astype(dtype)


def setup_inputs(seed: int = 0, part: int = 0) -> dict:
    keys = jax.random.split(jax.random.key(seed), 5)
    own_keys = jax.random.split(jax.random.fold_in(keys[4], part), 5)
    return {
        "spectra": scatter_about(own_keys[0], (C, 2 * SNAP), 0.7071, 6.0, ((0, 16),)),
        "loading": jnp.clip(jnp.exp(jax.random.uniform(own_keys[1], (C,), jnp.float32, math.log(0.05), math.log(0.5))), 0.05, 0.5),
        "delays": place_ends(jax.random.randint(keys[2], (C, NSLOW), 0, MAXDELAY), jax.random.fold_in(keys[2], 1), 0, MAXDELAY - 1).astype(jnp.int32),
        "bin_index": jax.random.randint(own_keys[3], (1,), 1, NFFT // 2).astype(jnp.int32),
    }


two_pi = 6.283185307179586

def lower_solve(factor, right_side):
    return jax.scipy.linalg.solve_triangular(factor, right_side, lower=True)

def reference(spectra, loading, delays, bin_index):
    csd_full = jnp.dot(spectra.astype(jnp.float32), spectra.T.astype(jnp.float32), preferred_element_type=jnp.float32) / SNAP + jnp.diag(loading)
    factor = jnp.linalg.cholesky(csd_full[:PANEL, :PANEL])
    panel = lower_solve(factor, csd_full[:, :PANEL].T).T
    update = csd_full - jnp.dot(panel.astype(jnp.float32), panel.T.astype(jnp.float32), precision=lax.Precision.HIGHEST, preferred_element_type=jnp.float32)
    keep_rows = jnp.arange(C) >= PANEL
    trailing = jnp.where(keep_rows[:, None] & keep_rows[None, :], update, 0.0)
    phase_int = delays * bin_index[0] % NFFT
    phase_angle = phase_int.astype(jnp.float32) * (two_pi / NFFT)
    steer_full = jnp.concatenate([jnp.cos(phase_angle), jnp.sin(phase_angle)], axis=1)
    solved = lower_solve(factor, steer_full[:PANEL])
    lower_rows = steer_full[PANEL:] - jnp.dot(panel[PANEL:].astype(jnp.float32), solved.astype(jnp.float32), precision=lax.Precision.HIGHEST, preferred_element_type=jnp.float32)
    stacked = jnp.concatenate([solved, lower_rows], axis=0)
    whitened = jnp.stack([stacked[:, :NSLOW], stacked[:, NSLOW:]])
    return (trailing, panel, whitened)
```

```python
import functools

import jax
import jax.numpy as jnp
from jax import lax
from jax.experimental import pallas as pl
from jax.experimental.pallas import tpu as pltpu
from jax.sharding import PartitionSpec as P

PANEL = 512
NFFT = 2048
BLK = 128
SUB = 8

two_pi = 6.283185307179586
F32 = jnp.float32
BF16 = jnp.bfloat16
HIGHEST = lax.Precision.HIGHEST
NT = (((1,), (1,)), ((), ()))


def dot_nt(a, b, precision=None):
    return lax.dot_general(a, b, NT, precision=precision, preferred_element_type=F32)


def split(x):
    high = x.astype(BF16)
    return high, (x - high.astype(F32)).astype(BF16)


def vmem(shape=None, index=None):
    if shape is None:
        return pl.BlockSpec(memory_space=pltpu.VMEM)
    return pl.BlockSpec(shape, index, memory_space=pltpu.VMEM)


SMEM = pl.BlockSpec(memory_space=pltpu.SMEM)
ANY = pl.BlockSpec(memory_space=pl.ANY)


def cost(flops, nbytes):
    return pl.CostEstimate(flops=int(flops), bytes_accessed=int(nbytes), transcendentals=0)


def lanes_of(x, j):
    return jnp.broadcast_to(x[:, j : j + 1], x.shape)


def rows_of(x, i):
    return jnp.broadcast_to(x[i : i + 1], x.shape)


def inverse_factor(block):
    n = block.shape[0]
    sub = lax.broadcasted_iota(jnp.int32, (SUB, n), 0)
    diagonal = lax.broadcasted_iota(jnp.int32, (n, n), 0) == lax.broadcasted_iota(jnp.int32, (n, n), 1)
    left = block
    right = jnp.where(diagonal, 1.0, 0.0).astype(F32)
    done = []
    for v in range(n // SUB):
        top, inv = left[:SUB], right[:SUB]
        columns = [lanes_of(top, SUB * v + k) for k in range(SUB)]
        for j in range(SUB):
            scale = lax.rsqrt(rows_of(columns[j], j))
            coef = columns[j] * scale
            for k in range(j + 1, SUB):
                columns[k] = columns[k] - coef * rows_of(coef, k)
            own_top, own_inv = rows_of(top, j) * scale, rows_of(inv, j) * scale
            top = jnp.where(sub == j, own_top, jnp.where(sub > j, top - coef * own_top, top))
            inv = jnp.where(sub == j, own_inv, jnp.where(sub > j, inv - coef * own_inv, inv))
        done.append(inv)
        if SUB * (v + 1) < n:
            below = jnp.transpose(top)[SUB * (v + 1) :, :]
            left = left[SUB:] - jnp.dot(below, top, precision=HIGHEST, preferred_element_type=F32)
            right = right[SUB:] - jnp.dot(below, inv, precision=HIGHEST, preferred_element_type=F32)
    return jnp.concatenate(done, axis=0)


def factor_kernel(snap, parts, spot_ref, *refs):
    pieces, (load_ref, inv_ref, head_ref, csd) = refs[:parts], refs[parts:]
    n = csd.shape[0]
    rows = n // parts
    for m, piece in enumerate(pieces):
        at = pl.multiple_of(jnp.bitwise_xor(spot_ref[0], m) * rows, rows)
        head_ref[pl.ds(at, rows), :] = piece[...]
    row = lax.broadcasted_iota(jnp.int32, (n, n), 0)
    col = lax.broadcasted_iota(jnp.int32, (n, n), 1)
    gram = dot_nt(head_ref[...], head_ref[...]) / snap
    csd[...] = gram + jnp.where(row == col, load_ref[...], 0.0)
    inv_ref[...] = jnp.where(row == col, 1.0, 0.0)
    below = lax.broadcasted_iota(jnp.int32, (n, BLK), 0)

    def step(k, _):
        at = pl.multiple_of(k * BLK, BLK)
        inv = inverse_factor(csd[pl.ds(at, BLK), pl.ds(at, BLK)])
        side = dot_nt(csd[:, pl.ds(at, BLK)], inv, HIGHEST)
        side = jnp.where(below >= at + BLK, side, 0.0)
        own = jnp.dot(inv, inv_ref[pl.ds(at, BLK), :], precision=HIGHEST, preferred_element_type=F32)
        inv_ref[pl.ds(at, BLK), :] = own
        inv_ref[...] -= jnp.dot(side, own, precision=HIGHEST, preferred_element_type=F32)
        csd[...] -= dot_nt(side, side, HIGHEST)
        return 0

    lax.fori_loop(0, n // BLK, step, 0)


def head_factor(spot, pieces, load, snap):
    depth = pieces[0].shape[1]
    n = load.shape[1]
    return pl.pallas_call(
        functools.partial(factor_kernel, snap, len(pieces)),
        out_shape=(jax.ShapeDtypeStruct((n, n), F32), jax.ShapeDtypeStruct((n, depth), BF16)),
        in_specs=[SMEM] + [vmem()] * (len(pieces) + 1),
        out_specs=(vmem(), vmem()),
        scratch_shapes=[pltpu.VMEM((n, n), F32)],
        compiler_params=pltpu.CompilerParams(vmem_limit_bytes=40 << 20),
        cost_estimate=cost(40e9, 4e6),
    )(spot, *pieces, load)


def panel_kernel(snap, spot_ref, rows_ref, head_ref, inv_ref, load_ref, panel_ref, high_ref, low_ref):
    side = dot_nt(rows_ref[...], head_ref[...]) / snap
    row = lax.broadcasted_iota(jnp.int32, side.shape, 0) + (spot_ref[0] + pl.program_id(0) * side.shape[0])
    side = side + jnp.where(row == lax.broadcasted_iota(jnp.int32, side.shape, 1), load_ref[...], 0.0)
    panel = dot_nt(side, inv_ref[...], HIGHEST)
    panel_ref[...] = panel
    high, low = split(panel)
    high_ref[...] = high
    low_ref[...] = low


def own_panel(first, rows, head, inv, load, snap, tile):
    n, depth = rows.shape
    width = head.shape[0]
    return pl.pallas_call(
        functools.partial(panel_kernel, snap),
        grid=(n // tile,),
        out_shape=tuple(jax.ShapeDtypeStruct((n, width), t) for t in (F32, BF16, BF16)),
        in_specs=[
            SMEM,
            vmem((tile, depth), lambda i: (i, 0)),
            vmem((width, depth), lambda i: (0, 0)),
            vmem((width, width), lambda i: (0, 0)),
            vmem((1, width), lambda i: (0, 0)),
        ],
        out_specs=tuple(vmem((tile, width), lambda i: (i, 0)) for _ in range(3)),
        compiler_params=pltpu.CompilerParams(vmem_limit_bytes=40 << 20),
        cost_estimate=cost(2 * n * width * (depth + 6 * width), 2 * n * depth + 8 * n * width),
    )(first, rows, head, inv, load)


def trailing_kernel(snap, geo, gather, spot_ref, *refs):
    tile, groups, width, stride, first, size = geo
    parts = 7 if gather else 1
    sources = refs[:parts]
    rows_ref, high_ref, low_ref, head_ref, inv_ref, load_ref = refs[parts : parts + 6]
    out_ref, cols_ref, col_high, col_low, acc, out_sem, in_sem = refs[len(refs) - 7 :]
    row_at, col_at = spot_ref[0], spot_ref[1]
    step, steps = pl.program_id(0), pl.num_programs(0)
    slot = lax.rem(step, 2)

    def out_copies(slot, step):
        at = pl.multiple_of(step * tile, tile)
        return [
            pltpu.make_async_copy(
                acc.at[slot, :, pl.ds(g * width, width)],
                out_ref.at[pl.ds(at, tile), pl.ds(g * stride + first, width)],
                out_sem.at[slot],
            )
            for g in range(groups)
        ]

    @pl.when(step == 0)
    def _():
        if gather:
            own, ups, downs = sources[0], sources[1:4], sources[4:7]
            piece = width // 4

            def pull(src, plane):
                for g in range(groups):
                    pltpu.make_async_copy(
                        src.at[pl.ds(g * piece, piece)],
                        cols_ref.at[pl.ds(pl.multiple_of(g * width + plane * piece, piece), piece)],
                        in_sem,
                    ).start()

            pull(own, row_at)
            for j in range(1, 4):

                @pl.when(row_at >= j)
                def _(j=j):
                    pull(ups[j - 1], row_at - j)

                @pl.when(row_at < j)
                def _(j=j):
                    pull(downs[3 - j], row_at - j + 4)

        else:
            pltpu.make_async_copy(sources[0], cols_ref, in_sem).start()
        pltpu.make_async_copy(cols_ref, cols_ref, in_sem).wait()
        side = dot_nt(cols_ref[...], head_ref[...]) / snap
        high, low = split(dot_nt(side, inv_ref[...], HIGHEST))
        col_high[...] = high
        col_low[...] = low

    @pl.when(step >= 2)
    def _():
        pltpu.make_async_copy(acc.at[slot], acc.at[slot], out_sem.at[slot]).wait()

    total = dot_nt(rows_ref[...], cols_ref[...]) / snap
    total -= dot_nt(high_ref[...], col_high[...])
    total -= dot_nt(high_ref[...], col_low[...])
    total -= dot_nt(low_ref[...], col_high[...])
    row = lax.broadcasted_iota(jnp.int32, (tile, width), 0) + (row_at * size + step * tile)
    for g in range(groups):
        col = lax.broadcasted_iota(jnp.int32, (tile, width), 1) + (col_at * size + g * stride + first)
        load = load_ref[0:1, g * stride + first : g * stride + first + width]
        mine = total[:, g * width : (g + 1) * width] + jnp.where(row == col, load, 0.0)
        acc[slot, :, g * width : (g + 1) * width] = jnp.where((row >= PANEL) & (col >= PANEL), mine, 0.0)
    for copy in out_copies(slot, step):
        copy.start()

    @pl.when(step == steps - 1)
    def _():
        for k in range(2):
            pltpu.make_async_copy(acc.at[k], acc.at[k], out_sem.at[k]).wait()


def trailing_part(spot, sources, rows, high, low, head, inv, load, so_far, snap, geo):
    tile, groups, width, stride, first, size = geo
    n, depth = rows.shape
    panel = head.shape[0]
    count = groups * width
    gather = len(sources) > 1
    given = [spot, *sources, rows, high, low, head, inv, load]
    specs = [SMEM] + [ANY] * len(sources) + [
        vmem((tile, depth), lambda i: (i, 0)),
        vmem((tile, panel), lambda i: (i, 0)),
        vmem((tile, panel), lambda i: (i, 0)),
        vmem((panel, depth), lambda i: (0, 0)),
        vmem((panel, panel), lambda i: (0, 0)),
        vmem((1, size), lambda i: (0, 0)),
    ]
    alias = {}
    if so_far is not None:
        alias = {len(given): 0}
        given.append(so_far)
        specs.append(ANY)
    return pl.pallas_call(
        functools.partial(trailing_kernel, snap, geo, gather),
        grid=(n // tile,),
        out_shape=jax.ShapeDtypeStruct((n, size), F32),
        in_specs=specs,
        out_specs=ANY,
        scratch_shapes=[
            pltpu.VMEM((count, depth), BF16),
            pltpu.VMEM((count, panel), BF16),
            pltpu.VMEM((count, panel), BF16),
            pltpu.VMEM((2, tile, count), F32),
            pltpu.SemaphoreType.DMA((2,)),
            pltpu.SemaphoreType.DMA,
        ],
        input_output_aliases=alias,
        compiler_params=pltpu.CompilerParams(vmem_limit_bytes=56 << 20),
        cost_estimate=cost(2 * n * count * (depth + 3 * panel), 2 * n * depth + 4 * n * count),
    )(*given)


def steer_kernel(spot_ref, steer_ref, top_ref, high_ref, low_ref, inv_ref, out_ref, solved):
    step = pl.program_id(0)
    tile = steer_ref.shape[0]

    @pl.when(step == 0)
    def _():
        solved[...] = jnp.dot(inv_ref[...], top_ref[...], precision=HIGHEST, preferred_element_type=F32)

    s_high, s_low = split(solved[...])
    below = steer_ref[...]
    below -= jnp.dot(high_ref[...], s_high, preferred_element_type=F32)
    below -= jnp.dot(high_ref[...], s_low, preferred_element_type=F32)
    below -= jnp.dot(low_ref[...], s_high, preferred_element_type=F32)
    half = below.shape[1] // 2
    out_ref[0] = below[:, :half]
    out_ref[1] = below[:, half:]

    @pl.when((spot_ref[0] == 0) & (step * tile < PANEL))
    def _():
        mine = solved[pl.ds(pl.multiple_of(step * tile, tile), tile), :]
        out_ref[0] = mine[:, :half]
        out_ref[1] = mine[:, half:]


def whiten(spot, steer, top, high, low, inv, tile):
    n, width = steer.shape
    panel = inv.shape[0]
    return pl.pallas_call(
        steer_kernel,
        grid=(n // tile,),
        out_shape=jax.ShapeDtypeStruct((2, n, width // 2), F32),
        in_specs=[
            SMEM,
            vmem((tile, width), lambda i: (i, 0)),
            vmem((panel, width), lambda i: (0, 0)),
            vmem((tile, panel), lambda i: (i, 0)),
            vmem((tile, panel), lambda i: (i, 0)),
            vmem((panel, panel), lambda i: (0, 0)),
        ],
        out_specs=vmem((2, tile, width // 2), lambda i: (0, i, 0)),
        scratch_shapes=[pltpu.VMEM((panel, width), F32)],
        compiler_params=pltpu.CompilerParams(vmem_limit_bytes=40 << 20),
        cost_estimate=cost(6 * n * panel * width, 8 * n * width + 4 * n * panel),
    )(spot, steer, top, high, low, inv)


def line_kernel(spot_ref, own, *refs):
    ups, downs, out, sem = refs[:3], refs[3:6], refs[6], refs[7]
    n = own.shape[0]
    at = spot_ref[0]

    def put(src, plane):
        pltpu.make_async_copy(src, out.at[pl.ds(pl.multiple_of(plane * n, n), n)], sem).start()

    put(own, at)
    for j in range(1, 4):

        @pl.when(at >= j)
        def _(j=j):
            put(ups[j - 1], at - j)

        @pl.when(at < j)
        def _(j=j):
            put(downs[3 - j], at - j + 4)

    pltpu.make_async_copy(out, out, sem).wait()


def in_line(spot, own, ups, downs):
    n, depth = own.shape
    return pl.pallas_call(
        line_kernel,
        out_shape=jax.ShapeDtypeStruct((4 * n, depth), own.dtype),
        in_specs=[SMEM] + [ANY] * 7,
        out_specs=ANY,
        scratch_shapes=[pltpu.SemaphoreType.DMA],
        cost_estimate=cost(0, 16 * n * depth),
    )(spot, own, *ups, *downs)


def steer_of(delays, bin_index):
    angle = (delays * bin_index % NFFT).astype(F32) * (two_pi / NFFT)
    return jnp.concatenate([jnp.cos(angle), jnp.sin(angle)], axis=1)


def planned(count):
    def move(value, pairs):
        return lax.ppermute(value, ("row", "col"), [(a * count + b, c * count + d) for (a, b), (c, d) in pairs])

    def across(m):
        return [((r, p), (r, p ^ m)) for r in range(count) for p in range(count)]

    def along(k, way):
        planes = [r for r in range(count) if 0 <= r + way < count and 0 <= r - way * (k - 1) < count]
        return [((r, p), (r + way, p)) for r in planes for p in range(count)]

    def line(own):
        ups, downs = [own], [own]
        for k in range(1, count):
            ups.append(move(ups[-1], along(k, 1)))
            downs.append(move(downs[-1], along(k, -1)))
        return ups[1:], downs[1:]

    def chosen(index, values):
        out = values[-1]
        for k in range(len(values) - 2, -1, -1):
            out = jnp.where(index == k, values[k], out)
        return out

    def on_device(spectra, loading, delays, bin_index):
        row, col = lax.axis_index("row"), lax.axis_index("col")
        block, depth = spectra.shape
        size = delays.shape[0]
        snap = depth // 2
        early = block * 3 // 5
        spot_row = row.astype(jnp.int32).reshape(1)
        spot = jnp.stack([row, col]).astype(jnp.int32)

        quarter = PANEL // count
        quarters = [lax.slice_in_dim(spectra, j * quarter, (j + 1) * quarter) for j in range(count)]
        held = chosen(col, [quarters[0]] + [move(quarters[j], [((0, 0), (0, j))]) for j in range(1, count)])
        lifted = [held] + [move(held, [((0, p), (k, p)) for p in range(count)]) for k in range(1, count)]
        piece = chosen(row, lifted)
        pieces = [piece] + [move(piece, across(m)) for m in range(1, count)]

        top = delays[:PANEL].astype(jnp.int16)
        tops = [top] + [move(top, [((0, p), (k, p)) for p in range(count)]) for k in range(1, count)]
        steer_top = steer_of(chosen(row, tops).astype(jnp.int32), bin_index[0])
        steer = steer_of(delays, bin_index[0])

        own_rows = lax.all_gather(spectra, "col", axis=0, tiled=True)

        first = spectra[:early]
        ups, downs = line(first)
        stacked = in_line(spot_row, first, ups, downs)
        cols_first = lax.all_to_all(stacked, "col", 0, 0, tiled=True)
        rest = lax.all_to_all(spectra[early:], "row", 0, 0, tiled=True)
        rest = lax.all_to_all(rest, "col", 0, 0, tiled=True)
        rest_ups, rest_downs = line(rest)

        head_load = loading[:PANEL].reshape(1, PANEL)
        inv, head = head_factor(col.astype(jnp.int32).reshape(1), pieces, head_load, snap)
        panel, high, low = own_panel(spot_row * size, own_rows, head, inv, head_load, snap, size // 10)
        whitened = whiten(spot_row, steer, steer_top, high, low, inv, PANEL // 2)

        load = lax.dynamic_slice_in_dim(loading, col * size, size).reshape(1, size)
        tile = size // 8
        trailing = trailing_part(
            spot, [cols_first], own_rows, high, low, head, inv, load, None, snap,
            (tile, count, early, block, 0, size),
        )
        trailing = trailing_part(
            spot, [rest, *rest_ups, *rest_downs], own_rows, high, low, head, inv, load, trailing, snap,
            (tile, count, block - early, block, early, size),
        )
        return (trailing, panel, whitened)

    return on_device


def from_root(value, axis, source):
    kept = jnp.where(lax.axis_index(axis) == source, value, 0).astype(value.dtype)
    return lax.psum(kept, axis)


def lower_solve(factor, right_side):
    return jax.scipy.linalg.solve_triangular(factor, right_side, lower=True)


def general(spectra, loading, delays, bin_index):
    row_index, col_index = lax.axis_index("row"), lax.axis_index("col")
    size, slow_count = delays.shape
    snap = spectra.shape[1] // 2
    own_rows = lax.all_gather(spectra, "col", axis=0, tiled=True)
    col_rows = from_root(own_rows, "row", col_index)
    row_load = lax.dynamic_slice_in_dim(loading, row_index * size, size)
    tile_csd = jnp.dot(own_rows, col_rows.T, preferred_element_type=F32) / snap
    tile_csd = tile_csd + jnp.where(row_index == col_index, jnp.diag(row_load), 0.0)
    head_rows = from_root(own_rows[:PANEL], "row", 0)
    head_csd = jnp.dot(head_rows, head_rows.T, preferred_element_type=F32) / snap
    factor = jnp.linalg.cholesky(head_csd + jnp.diag(loading[:PANEL]))
    head_load = jnp.eye(size, PANEL, dtype=F32) * loading[:PANEL][None, :]
    own_side = jnp.dot(own_rows, head_rows.T, preferred_element_type=F32) / snap
    own_side = own_side + jnp.where(row_index == 0, head_load, 0.0)
    col_side = jnp.dot(col_rows, head_rows.T, preferred_element_type=F32) / snap
    col_side = col_side + jnp.where(col_index == 0, head_load, 0.0)
    panel = lower_solve(factor, own_side.T).T
    col_panel = lower_solve(factor, col_side.T).T
    glob_rows = row_index * size + jnp.arange(size)
    glob_cols = col_index * size + jnp.arange(size)
    update = tile_csd - jnp.dot(panel, col_panel.T, precision=HIGHEST, preferred_element_type=F32)
    trailing = jnp.where((glob_rows[:, None] >= PANEL) & (glob_cols[None, :] >= PANEL), update, 0.0)
    steer = steer_of(delays, bin_index[0])
    solved = from_root(lower_solve(factor, steer[:PANEL]), "row", 0)
    lower_rows = steer - jnp.dot(panel, solved, precision=HIGHEST, preferred_element_type=F32)
    padded = jnp.pad(solved, ((0, size - PANEL), (0, 0)))
    stacked = jnp.where(glob_rows[:, None] < PANEL, padded, lower_rows)
    whitened = jnp.stack([stacked[:, :slow_count], stacked[:, slow_count:]])
    return (trailing, panel, whitened)


def solution(mesh):
    count = mesh.shape["col"]
    square = mesh.shape["row"] == count
    return jax.shard_map(
        planned(count) if square and count == 4 else general,
        mesh=mesh,
        in_specs=(P(("row", "col"), "freq"), P("freq"), P("row", "col"), P("freq")),
        out_specs=(
            P(("freq", "row"), "col"),
            P(("freq", "row"), None),
            P(None, ("freq", "row"), "col"),
        ),
        check_vma=False,
    )
```

```python
import functools

import jax
import jax.numpy as jnp
from jax import lax
from jax.experimental import pallas as pl
from jax.experimental.pallas import tpu as pltpu
from jax.sharding import PartitionSpec as P

PANEL = 512
NFFT = 2048
BLK = 128
SUB = 8

two_pi = 6.283185307179586
F32 = jnp.float32
BF16 = jnp.bfloat16
HIGHEST = lax.Precision.HIGHEST
NT = (((1,), (1,)), ((), ()))


def dot_nt(a, b, precision=None):
    return lax.dot_general(a, b, NT, precision=precision, preferred_element_type=F32)


def split(x):
    high = x.astype(BF16)
    return high, (x - high.astype(F32)).astype(BF16)


def vmem(shape=None, index=None):
    if shape is None:
        return pl.BlockSpec(memory_space=pltpu.VMEM)
    return pl.BlockSpec(shape, index, memory_space=pltpu.VMEM)


SMEM = pl.BlockSpec(memory_space=pltpu.SMEM)
ANY = pl.BlockSpec(memory_space=pl.ANY)


def cost(flops, nbytes):
    return pl.CostEstimate(flops=int(flops), bytes_accessed=int(nbytes), transcendentals=0)


def lanes_of(x, j):
    return jnp.broadcast_to(x[:, j : j + 1], x.shape)


def rows_of(x, i):
    return jnp.broadcast_to(x[i : i + 1], x.shape)


def inverse_factor(block):
    n = block.shape[0]
    sub = lax.broadcasted_iota(jnp.int32, (SUB, n), 0)
    diagonal = lax.broadcasted_iota(jnp.int32, (n, n), 0) == lax.broadcasted_iota(jnp.int32, (n, n), 1)
    left = block
    right = jnp.where(diagonal, 1.0, 0.0).astype(F32)
    done = []
    for v in range(n // SUB):
        top, inv = left[:SUB], right[:SUB]
        columns = [lanes_of(top, SUB * v + k) for k in range(SUB)]
        for j in range(SUB):
            scale = lax.rsqrt(rows_of(columns[j], j))
            coef = columns[j] * scale
            for k in range(j + 1, SUB):
                columns[k] = columns[k] - coef * rows_of(coef, k)
            own_top, own_inv = rows_of(top, j) * scale, rows_of(inv, j) * scale
            top = jnp.where(sub == j, own_top, jnp.where(sub > j, top - coef * own_top, top))
            inv = jnp.where(sub == j, own_inv, jnp.where(sub > j, inv - coef * own_inv, inv))
        done.append(inv)
        if SUB * (v + 1) < n:
            below = jnp.transpose(top)[SUB * (v + 1) :, :]
            left = left[SUB:] - jnp.dot(below, top, precision=HIGHEST, preferred_element_type=F32)
            right = right[SUB:] - jnp.dot(below, inv, precision=HIGHEST, preferred_element_type=F32)
    return jnp.concatenate(done, axis=0)


def factor_kernel(snap, parts, spot_ref, *refs):
    pieces, (load_ref, inv_ref, head_ref, csd) = refs[:parts], refs[parts:]
    n = csd.shape[0]
    rows = n // parts
    for m, piece in enumerate(pieces):
        at = pl.multiple_of(jnp.bitwise_xor(spot_ref[0], m) * rows, rows)
        head_ref[pl.ds(at, rows), :] = piece[...]
    row = lax.broadcasted_iota(jnp.int32, (n, n), 0)
    col = lax.broadcasted_iota(jnp.int32, (n, n), 1)
    gram = dot_nt(head_ref[...], head_ref[...]) / snap
    csd[...] = gram + jnp.where(row == col, load_ref[...], 0.0)
    inv_ref[...] = jnp.where(row == col, 1.0, 0.0)
    below = lax.broadcasted_iota(jnp.int32, (n, BLK), 0)

    def step(k, _):
        at = pl.multiple_of(k * BLK, BLK)
        inv = inverse_factor(csd[pl.ds(at, BLK), pl.ds(at, BLK)])
        side = dot_nt(csd[:, pl.ds(at, BLK)], inv, HIGHEST)
        side = jnp.where(below >= at + BLK, side, 0.0)
        own = jnp.dot(inv, inv_ref[pl.ds(at, BLK), :], precision=HIGHEST, preferred_element_type=F32)
        inv_ref[pl.ds(at, BLK), :] = own
        inv_ref[...] -= jnp.dot(side, own, precision=HIGHEST, preferred_element_type=F32)
        csd[...] -= dot_nt(side, side, HIGHEST)
        return 0

    lax.fori_loop(0, n // BLK, step, 0)


def head_factor(spot, pieces, load, snap):
    depth = pieces[0].shape[1]
    n = load.shape[1]
    return pl.pallas_call(
        functools.partial(factor_kernel, snap, len(pieces)),
        out_shape=(jax.ShapeDtypeStruct((n, n), F32), jax.ShapeDtypeStruct((n, depth), BF16)),
        in_specs=[SMEM] + [vmem()] * (len(pieces) + 1),
        out_specs=(vmem(), vmem()),
        scratch_shapes=[pltpu.VMEM((n, n), F32)],
        compiler_params=pltpu.CompilerParams(vmem_limit_bytes=40 << 20),
        cost_estimate=cost(40e9, 4e6),
    )(spot, *pieces, load)


def panel_kernel(snap, spot_ref, rows_ref, head_ref, inv_ref, load_ref, steer_ref, top_ref, *refs):
    panel_ref, high_ref, low_ref, white_ref, solved = refs
    step = pl.program_id(0)
    tile = rows_ref.shape[0]

    @pl.when(step == 0)
    def _():
        solved[...] = jnp.dot(inv_ref[...], top_ref[...], precision=HIGHEST, preferred_element_type=F32)

    side = dot_nt(rows_ref[...], head_ref[...]) / snap
    row = lax.broadcasted_iota(jnp.int32, side.shape, 0) + (spot_ref[0] * (tile * pl.num_programs(0)) + step * tile)
    side = side + jnp.where(row == lax.broadcasted_iota(jnp.int32, side.shape, 1), load_ref[...], 0.0)
    panel = dot_nt(side, inv_ref[...], HIGHEST)
    panel_ref[...] = panel
    high, low = split(panel)
    high_ref[...] = high
    low_ref[...] = low
    s_high, s_low = split(solved[...])
    below = steer_ref[...]
    below -= jnp.dot(high, s_high, preferred_element_type=F32)
    below -= jnp.dot(high, s_low, preferred_element_type=F32)
    below -= jnp.dot(low, s_high, preferred_element_type=F32)
    half = below.shape[1] // 2
    white_ref[0] = below[:, :half]
    white_ref[1] = below[:, half:]

    @pl.when((spot_ref[0] == 0) & (step * tile < PANEL))
    def _():
        mine = solved[pl.ds(pl.multiple_of(step * tile, tile), tile), :]
        white_ref[0] = mine[:, :half]
        white_ref[1] = mine[:, half:]


def own_panel(spot, rows, head, inv, load, steer, top, snap, tile):
    n, depth = rows.shape
    width = head.shape[0]
    vectors = steer.shape[1]
    return pl.pallas_call(
        functools.partial(panel_kernel, snap),
        grid=(n // tile,),
        out_shape=tuple(jax.ShapeDtypeStruct((n, width), t) for t in (F32, BF16, BF16))
        + (jax.ShapeDtypeStruct((2, n, vectors // 2), F32),),
        in_specs=[
            SMEM,
            vmem((tile, depth), lambda i: (i, 0)),
            vmem((width, depth), lambda i: (0, 0)),
            vmem((width, width), lambda i: (0, 0)),
            vmem((1, width), lambda i: (0, 0)),
            vmem((tile, vectors), lambda i: (i, 0)),
            vmem((width, vectors), lambda i: (0, 0)),
        ],
        out_specs=tuple(vmem((tile, width), lambda i: (i, 0)) for _ in range(3))
        + (vmem((2, tile, vectors // 2), lambda i: (0, i, 0)),),
        scratch_shapes=[pltpu.VMEM((width, vectors), F32)],
        compiler_params=pltpu.CompilerParams(vmem_limit_bytes=48 << 20),
        cost_estimate=cost(2 * n * width * (depth + 6 * width), 2 * n * depth + 8 * n * width),
    )(spot, rows, head, inv, load, steer, top)


def trailing_kernel(snap, geo, gather, spot_ref, *refs):
    tile, groups, width, stride, first, size = geo
    source = refs[0]
    rows_ref, high_ref, low_ref, head_ref, inv_ref, load_ref = refs[1:7]
    out_ref, cols_ref, col_high, col_low, acc, out_sem, in_sem = refs[len(refs) - 7 :]
    row_at, col_at = spot_ref[0], spot_ref[1]
    step, steps = pl.program_id(0), pl.num_programs(0)
    slot = lax.rem(step, 2)

    def out_copies(slot, step):
        at = pl.multiple_of(step * tile, tile)
        return [
            pltpu.make_async_copy(
                acc.at[slot, :, pl.ds(g * width, width)],
                out_ref.at[pl.ds(at, tile), pl.ds(g * stride + first, width)],
                out_sem.at[slot],
            )
            for g in range(groups)
        ]

    @pl.when(step == 0)
    def _():
        piece = width // groups
        for g in range(groups):
            if gather:
                for k in range(groups):
                    pltpu.make_async_copy(
                        source.at[pl.ds((k * groups + g) * piece, piece)],
                        cols_ref.at[pl.ds(g * width + k * piece, piece)],
                        in_sem.at[g],
                    ).start()
            else:
                part = pl.ds(g * width, width)
                pltpu.make_async_copy(source.at[part], cols_ref.at[part], in_sem.at[g]).start()
        for g in range(groups):
            part = pl.ds(g * width, width)
            pltpu.make_async_copy(cols_ref.at[part], cols_ref.at[part], in_sem.at[g]).wait()
            side = dot_nt(cols_ref[part, :], head_ref[...]) / snap
            high, low = split(dot_nt(side, inv_ref[...], HIGHEST))
            col_high[part, :] = high
            col_low[part, :] = low

    @pl.when(step >= 2)
    def _():
        pltpu.make_async_copy(acc.at[slot], acc.at[slot], out_sem.at[slot]).wait()

    total = dot_nt(rows_ref[...], cols_ref[...]) / snap
    total -= dot_nt(high_ref[...], col_high[...])
    total -= dot_nt(high_ref[...], col_low[...])
    total -= dot_nt(low_ref[...], col_high[...])
    row = lax.broadcasted_iota(jnp.int32, (tile, width), 0) + (row_at * size + step * tile)
    for g in range(groups):
        col = lax.broadcasted_iota(jnp.int32, (tile, width), 1) + (col_at * size + g * stride + first)
        load = load_ref[0:1, g * stride + first : g * stride + first + width]
        mine = total[:, g * width : (g + 1) * width] + jnp.where(row == col, load, 0.0)
        acc[slot, :, g * width : (g + 1) * width] = jnp.where((row >= PANEL) & (col >= PANEL), mine, 0.0)
    for copy in out_copies(slot, step):
        copy.start()

    @pl.when(step == steps - 1)
    def _():
        for k in range(2):
            pltpu.make_async_copy(acc.at[k], acc.at[k], out_sem.at[k]).wait()


def trailing_part(spot, source, gather, rows, high, low, head, inv, load, so_far, snap, geo):
    tile, groups, width, stride, first, size = geo
    n, depth = rows.shape
    panel = head.shape[0]
    count = groups * width
    given = [spot, source, rows, high, low, head, inv, load]
    specs = [SMEM, ANY,
        vmem((tile, depth), lambda i: (i, 0)),
        vmem((tile, panel), lambda i: (i, 0)),
        vmem((tile, panel), lambda i: (i, 0)),
        vmem((panel, depth), lambda i: (0, 0)),
        vmem((panel, panel), lambda i: (0, 0)),
        vmem((1, size), lambda i: (0, 0)),
    ]
    alias = {}
    if so_far is not None:
        alias = {len(given): 0}
        given.append(so_far)
        specs.append(ANY)
    return pl.pallas_call(
        functools.partial(trailing_kernel, snap, geo, gather),
        grid=(n // tile,),
        out_shape=jax.ShapeDtypeStruct((n, size), F32),
        in_specs=specs,
        out_specs=ANY,
        scratch_shapes=[
            pltpu.VMEM((count, depth), BF16),
            pltpu.VMEM((count, panel), BF16),
            pltpu.VMEM((count, panel), BF16),
            pltpu.VMEM((2, tile, count), F32),
            pltpu.SemaphoreType.DMA((2,)),
            pltpu.SemaphoreType.DMA((groups,)),
        ],
        input_output_aliases=alias,
        compiler_params=pltpu.CompilerParams(vmem_limit_bytes=56 << 20),
        cost_estimate=cost(2 * n * count * (depth + 3 * panel), 2 * n * depth + 4 * n * count),
    )(*given)


def line_kernel(spot_ref, own, *refs):
    ups, downs, out, held, in_sem, out_sem = refs[:3], refs[3:6], refs[6], refs[7], refs[8], refs[9]
    n = own.shape[0]
    at = spot_ref[0]

    def pull(src, k):
        pltpu.make_async_copy(src, held.at[k], in_sem.at[k]).start()

    pull(own, 0)
    for j in range(1, 4):

        @pl.when(at >= j)
        def _(j=j):
            pull(ups[j - 1], j)

        @pl.when(at < j)
        def _(j=j):
            pull(downs[3 - j], j)

    pushes = []
    for j in range(4):
        pltpu.make_async_copy(held.at[j], held.at[j], in_sem.at[j]).wait()
        plane = jnp.where(at >= j, at - j, at - j + 4)
        push = pltpu.make_async_copy(held.at[j], out.at[pl.ds(pl.multiple_of(plane * n, n), n)], out_sem.at[j])
        push.start()
        pushes.append(push)
    for push in pushes:
        push.wait()


def in_line(spot, own, ups, downs):
    n, depth = own.shape
    return pl.pallas_call(
        line_kernel,
        out_shape=jax.ShapeDtypeStruct((4 * n, depth), own.dtype),
        in_specs=[SMEM] + [ANY] * 7,
        out_specs=ANY,
        scratch_shapes=[
            pltpu.VMEM((4, n, depth), own.dtype),
            pltpu.SemaphoreType.DMA((4,)),
            pltpu.SemaphoreType.DMA((4,)),
        ],
        compiler_params=pltpu.CompilerParams(vmem_limit_bytes=24 << 20),
        cost_estimate=cost(0, 16 * n * depth),
    )(spot, own, *ups, *downs)


def after(value, *others):
    return lax.optimization_barrier((value, *others))[0]


def steer_of(delays, bin_index):
    angle = (delays * bin_index % NFFT).astype(F32) * (two_pi / NFFT)
    return jnp.concatenate([jnp.cos(angle), jnp.sin(angle)], axis=1)


def planned(count):
    def move(value, pairs):
        return lax.ppermute(value, ("row", "col"), [(a * count + b, c * count + d) for (a, b), (c, d) in pairs])

    def across(m):
        return [((r, p), (r, p ^ m)) for r in range(count) for p in range(count)]

    def along(k, way):
        planes = [r for r in range(count) if 0 <= r + way < count and 0 <= r - way * (k - 1) < count]
        return [((r, p), (r + way, p)) for r in planes for p in range(count)]

    def hop(value, k):
        return [move(value[0], along(k, 1)), move(value[1], along(k, -1))]

    def chosen(index, values):
        out = values[-1]
        for k in range(len(values) - 2, -1, -1):
            out = jnp.where(index == k, values[k], out)
        return out

    def on_device(spectra, loading, delays, bin_index):
        row, col = lax.axis_index("row"), lax.axis_index("col")
        block, depth = spectra.shape
        size = delays.shape[0]
        snap = depth // 2
        early = block * 3 // 5
        spot_row = row.astype(jnp.int32).reshape(1)
        spot = jnp.stack([row, col]).astype(jnp.int32)

        quarter = PANEL // count
        quarters = [lax.slice_in_dim(spectra, j * quarter, (j + 1) * quarter) for j in range(count)]
        first = spectra[:early]
        head_load = loading[:PANEL].reshape(1, PANEL)

        own_rows = lax.all_gather(spectra, "col", axis=0, tiled=True)
        one = hop([first, first], 1)
        held = chosen(col, [quarters[0]] + [move(quarters[j], [((0, 0), (0, j))]) for j in range(1, count)])
        top = delays[:PANEL].astype(jnp.int16)
        tops = [top] + [move(top, [((0, p), (k, p)) for p in range(count)]) for k in range(1, count)]

        held = after(held, *one, *tops)
        lifted = [held] + [move(held, [((0, p), (k, p)) for p in range(count)]) for k in range(1, count)]
        two = hop([after(v, held) for v in one], 2)
        rest = lax.all_to_all(after(spectra[early:], held), "row", 0, 0, tiled=True)
        piece = after(chosen(row, lifted), *two)

        pieces = [piece] + [move(piece, across(m)) for m in range(1, count)]
        three = hop([after(v, piece) for v in two], 3)
        rest = lax.all_to_all(after(rest, piece), "col", 0, 0, tiled=True)
        three = [after(v, *pieces) for v in three]
        stacked = in_line(spot_row, first, [one[0], two[0], three[0]], [one[1], two[1], three[1]])
        cols_first = lax.all_to_all(stacked, "col", 0, 0, tiled=True)
        cols_rest = lax.all_gather(after(rest, stacked), "row", axis=0, tiled=True)

        pieces = [after(v, stacked) for v in pieces]
        inv, head = head_factor(col.astype(jnp.int32).reshape(1), pieces, head_load, snap)
        steer_top = steer_of(chosen(row, tops).astype(jnp.int32), bin_index[0])
        steer = steer_of(delays, bin_index[0])
        panel, high, low, whitened = own_panel(
            spot_row, after(own_rows, rest), head, inv, head_load, steer, steer_top, snap, PANEL
        )

        load = lax.dynamic_slice_in_dim(loading, col * size, size).reshape(1, size)
        tile = size // 8
        trailing = trailing_part(
            spot, cols_first, False, own_rows, high, low, head, inv, load, None, snap,
            (tile, count, early, block, 0, size),
        )
        trailing = trailing_part(
            spot, cols_rest, True, own_rows, high, low, head, inv, load, trailing, snap,
            (tile, count, block - early, block, early, size),
        )
        return (trailing, panel, whitened)

    return on_device


def from_root(value, axis, source):
    kept = jnp.where(lax.axis_index(axis) == source, value, 0).astype(value.dtype)
    return lax.psum(kept, axis)


def lower_solve(factor, right_side):
    return jax.scipy.linalg.solve_triangular(factor, right_side, lower=True)


def general(spectra, loading, delays, bin_index):
    row_index, col_index = lax.axis_index("row"), lax.axis_index("col")
    size, slow_count = delays.shape
    snap = spectra.shape[1] // 2
    own_rows = lax.all_gather(spectra, "col", axis=0, tiled=True)
    col_rows = from_root(own_rows, "row", col_index)
    row_load = lax.dynamic_slice_in_dim(loading, row_index * size, size)
    tile_csd = jnp.dot(own_rows, col_rows.T, preferred_element_type=F32) / snap
    tile_csd = tile_csd + jnp.where(row_index == col_index, jnp.diag(row_load), 0.0)
    head_rows = from_root(own_rows[:PANEL], "row", 0)
    head_csd = jnp.dot(head_rows, head_rows.T, preferred_element_type=F32) / snap
    factor = jnp.linalg.cholesky(head_csd + jnp.diag(loading[:PANEL]))
    head_load = jnp.eye(size, PANEL, dtype=F32) * loading[:PANEL][None, :]
    own_side = jnp.dot(own_rows, head_rows.T, preferred_element_type=F32) / snap
    own_side = own_side + jnp.where(row_index == 0, head_load, 0.0)
    col_side = jnp.dot(col_rows, head_rows.T, preferred_element_type=F32) / snap
    col_side = col_side + jnp.where(col_index == 0, head_load, 0.0)
    panel = lower_solve(factor, own_side.T).T
    col_panel = lower_solve(factor, col_side.T).T
    glob_rows = row_index * size + jnp.arange(size)
    glob_cols = col_index * size + jnp.arange(size)
    update = tile_csd - jnp.dot(panel, col_panel.T, precision=HIGHEST, preferred_element_type=F32)
    trailing = jnp.where((glob_rows[:, None] >= PANEL) & (glob_cols[None, :] >= PANEL), update, 0.0)
    steer = steer_of(delays, bin_index[0])
    solved = from_root(lower_solve(factor, steer[:PANEL]), "row", 0)
    lower_rows = steer - jnp.dot(panel, solved, precision=HIGHEST, preferred_element_type=F32)
    padded = jnp.pad(solved, ((0, size - PANEL), (0, 0)))
    stacked = jnp.where(glob_rows[:, None] < PANEL, padded, lower_rows)
    whitened = jnp.stack([stacked[:, :slow_count], stacked[:, slow_count:]])
    return (trailing, panel, whitened)


def solution(mesh):
    count = mesh.shape["col"]
    square = mesh.shape["row"] == count
    return jax.shard_map(
        planned(count) if square and count == 4 else general,
        mesh=mesh,
        in_specs=(P(("row", "col"), "freq"), P("freq"), P("row", "col"), P("freq")),
        out_specs=(
            P(("freq", "row"), "col"),
            P(("freq", "row"), None),
            P(None, ("freq", "row"), "col"),
        ),
        check_vma=False,
    )
```

```python
import functools

import jax
import jax.numpy as jnp
from jax import lax
from jax.experimental import pallas as pl
from jax.experimental.pallas import tpu as pltpu
from jax.sharding import PartitionSpec as P

PANEL = 512
NFFT = 2048
BLK = 128
SUB = 16

two_pi = 6.283185307179586
F32 = jnp.float32
BF16 = jnp.bfloat16
HIGHEST = lax.Precision.HIGHEST
NT = (((1,), (1,)), ((), ()))


def dot_nt(a, b, precision=None):
    return lax.dot_general(a, b, NT, precision=precision, preferred_element_type=F32)


def split(x):
    high = x.astype(BF16)
    return high, (x - high.astype(F32)).astype(BF16)


def vmem(shape=None, index=None):
    if shape is None:
        return pl.BlockSpec(memory_space=pltpu.VMEM)
    return pl.BlockSpec(shape, index, memory_space=pltpu.VMEM)


SMEM = pl.BlockSpec(memory_space=pltpu.SMEM)
ANY = pl.BlockSpec(memory_space=pl.ANY)


def cost(flops, nbytes):
    return pl.CostEstimate(flops=int(flops), bytes_accessed=int(nbytes), transcendentals=0)


def lanes_of(x, j):
    return jnp.broadcast_to(x[:, j : j + 1], x.shape)


def rows_of(x, i):
    return jnp.broadcast_to(x[i : i + 1], x.shape)


def inverse_factor(block):
    n = block.shape[0]
    sub = lax.broadcasted_iota(jnp.int32, (SUB, n), 0)
    diagonal = lax.broadcasted_iota(jnp.int32, (n, n), 0) == lax.broadcasted_iota(jnp.int32, (n, n), 1)
    left = block
    right = jnp.where(diagonal, 1.0, 0.0).astype(F32)
    done = []
    for v in range(n // SUB):
        top, inv = left[:SUB], right[:SUB]
        columns = [lanes_of(top, SUB * v + k) for k in range(SUB)]
        for j in range(SUB):
            scale = lax.rsqrt(rows_of(columns[j], j))
            coef = columns[j] * scale
            for k in range(j + 1, SUB):
                columns[k] = columns[k] - coef * rows_of(coef, k)
            own_top, own_inv = rows_of(top, j) * scale, rows_of(inv, j) * scale
            top = jnp.where(sub == j, own_top, jnp.where(sub > j, top - coef * own_top, top))
            inv = jnp.where(sub == j, own_inv, jnp.where(sub > j, inv - coef * own_inv, inv))
        done.append(inv)
        if SUB * (v + 1) < n:
            below = jnp.transpose(top)[SUB * (v + 1) :, :]
            left = left[SUB:] - jnp.dot(below, top, precision=HIGHEST, preferred_element_type=F32)
            right = right[SUB:] - jnp.dot(below, inv, precision=HIGHEST, preferred_element_type=F32)
    return jnp.concatenate(done, axis=0)


def factor_kernel(snap, parts, spot_ref, *refs):
    pieces, (load_ref, inv_ref, head_ref, csd) = refs[:parts], refs[parts:]
    n = csd.shape[0]
    rows = n // parts
    for m, piece in enumerate(pieces):
        at = pl.multiple_of(jnp.bitwise_xor(spot_ref[0], m) * rows, rows)
        head_ref[pl.ds(at, rows), :] = piece[...]
    row = lax.broadcasted_iota(jnp.int32, (n, n), 0)
    col = lax.broadcasted_iota(jnp.int32, (n, n), 1)
    gram = dot_nt(head_ref[...], head_ref[...]) / snap
    csd[...] = gram + jnp.where(row == col, load_ref[...], 0.0)
    inv_ref[...] = jnp.where(row == col, 1.0, 0.0)
    for at in range(0, n, BLK):
        end = at + BLK
        inv = inverse_factor(csd[at:end, at:end])
        own = jnp.dot(inv, inv_ref[at:end, :end], precision=HIGHEST, preferred_element_type=F32)
        inv_ref[at:end, :end] = own
        if end < n:
            side = dot_nt(csd[end:, at:end], inv, HIGHEST)
            csd[end:, end:] -= dot_nt(side, side, HIGHEST)
            inv_ref[end:, :end] -= jnp.dot(side, own, precision=HIGHEST, preferred_element_type=F32)


def head_factor(spot, pieces, load, snap):
    depth = pieces[0].shape[1]
    n = load.shape[1]
    return pl.pallas_call(
        functools.partial(factor_kernel, snap, len(pieces)),
        out_shape=(jax.ShapeDtypeStruct((n, n), F32), jax.ShapeDtypeStruct((n, depth), BF16)),
        in_specs=[SMEM] + [vmem()] * (len(pieces) + 1),
        out_specs=(vmem(), vmem()),
        scratch_shapes=[pltpu.VMEM((n, n), F32)],
        compiler_params=pltpu.CompilerParams(vmem_limit_bytes=40 << 20),
        cost_estimate=cost(40e9, 4e6),
    )(spot, *pieces, load)


def panel_kernel(snap, spot_ref, rows_ref, head_ref, inv_ref, load_ref, steer_ref, top_ref, *refs):
    panel_ref, high_ref, low_ref, white_ref, solved = refs
    step = pl.program_id(0)
    tile = rows_ref.shape[0]

    @pl.when(step == 0)
    def _():
        solved[...] = jnp.dot(inv_ref[...], top_ref[...], precision=HIGHEST, preferred_element_type=F32)

    side = dot_nt(rows_ref[...], head_ref[...]) / snap
    row = lax.broadcasted_iota(jnp.int32, side.shape, 0) + (spot_ref[0] * (tile * pl.num_programs(0)) + step * tile)
    side = side + jnp.where(row == lax.broadcasted_iota(jnp.int32, side.shape, 1), load_ref[...], 0.0)
    panel = dot_nt(side, inv_ref[...], HIGHEST)
    panel_ref[...] = panel
    high, low = split(panel)
    high_ref[...] = high
    low_ref[...] = low
    s_high, s_low = split(solved[...])
    below = steer_ref[...]
    below -= jnp.dot(high, s_high, preferred_element_type=F32)
    below -= jnp.dot(high, s_low, preferred_element_type=F32)
    below -= jnp.dot(low, s_high, preferred_element_type=F32)
    half = below.shape[1] // 2
    white_ref[0] = below[:, :half]
    white_ref[1] = below[:, half:]

    @pl.when((spot_ref[0] == 0) & (step * tile < PANEL))
    def _():
        mine = solved[pl.ds(pl.multiple_of(step * tile, tile), tile), :]
        white_ref[0] = mine[:, :half]
        white_ref[1] = mine[:, half:]


def own_panel(spot, rows, head, inv, load, steer, top, snap, tile):
    n, depth = rows.shape
    width = head.shape[0]
    vectors = steer.shape[1]
    return pl.pallas_call(
        functools.partial(panel_kernel, snap),
        grid=(n // tile,),
        out_shape=tuple(jax.ShapeDtypeStruct((n, width), t) for t in (F32, BF16, BF16))
        + (jax.ShapeDtypeStruct((2, n, vectors // 2), F32),),
        in_specs=[
            SMEM,
            vmem((tile, depth), lambda i: (i, 0)),
            vmem((width, depth), lambda i: (0, 0)),
            vmem((width, width), lambda i: (0, 0)),
            vmem((1, width), lambda i: (0, 0)),
            vmem((tile, vectors), lambda i: (i, 0)),
            vmem((width, vectors), lambda i: (0, 0)),
        ],
        out_specs=tuple(vmem((tile, width), lambda i: (i, 0)) for _ in range(3))
        + (vmem((2, tile, vectors // 2), lambda i: (0, i, 0)),),
        scratch_shapes=[pltpu.VMEM((width, vectors), F32)],
        compiler_params=pltpu.CompilerParams(vmem_limit_bytes=48 << 20),
        cost_estimate=cost(2 * n * width * (depth + 6 * width), 2 * n * depth + 8 * n * width),
    )(spot, rows, head, inv, load, steer, top)


def trailing_kernel(snap, geo, gather, spot_ref, *refs):
    tile, groups, width, stride, first, size = geo
    source = refs[0]
    rows_ref, high_ref, low_ref, head_ref, inv_ref, load_ref = refs[1:7]
    out_ref, cols_ref, col_high, col_low, acc, out_sem, in_sem = refs[len(refs) - 7 :]
    row_at, col_at = spot_ref[0], spot_ref[1]
    step, steps = pl.program_id(0), pl.num_programs(0)
    slot = lax.rem(step, 2)

    def out_copies(slot, step):
        at = pl.multiple_of(step * tile, tile)
        return [
            pltpu.make_async_copy(
                acc.at[slot, :, pl.ds(g * width, width)],
                out_ref.at[pl.ds(at, tile), pl.ds(g * stride + first, width)],
                out_sem.at[slot],
            )
            for g in range(groups)
        ]

    @pl.when(step == 0)
    def _():
        piece = width // groups
        for g in range(groups):
            if gather:
                for k in range(groups):
                    pltpu.make_async_copy(
                        source.at[pl.ds((k * groups + g) * piece, piece)],
                        cols_ref.at[pl.ds(g * width + k * piece, piece)],
                        in_sem.at[g],
                    ).start()
            else:
                part = pl.ds(g * width, width)
                pltpu.make_async_copy(source.at[part], cols_ref.at[part], in_sem.at[g]).start()
        for g in range(groups):
            part = pl.ds(g * width, width)
            pltpu.make_async_copy(cols_ref.at[part], cols_ref.at[part], in_sem.at[g]).wait()
            side = dot_nt(cols_ref[part, :], head_ref[...]) / snap
            high, low = split(dot_nt(side, inv_ref[...], HIGHEST))
            col_high[part, :] = high
            col_low[part, :] = low

    @pl.when(step >= 2)
    def _():
        pltpu.make_async_copy(acc.at[slot], acc.at[slot], out_sem.at[slot]).wait()

    total = dot_nt(rows_ref[...], cols_ref[...]) / snap
    total -= dot_nt(high_ref[...], col_high[...])
    total -= dot_nt(high_ref[...], col_low[...])
    total -= dot_nt(low_ref[...], col_high[...])
    row = lax.broadcasted_iota(jnp.int32, (tile, width), 0) + (row_at * size + step * tile)
    for g in range(groups):
        col = lax.broadcasted_iota(jnp.int32, (tile, width), 1) + (col_at * size + g * stride + first)
        load = load_ref[0:1, g * stride + first : g * stride + first + width]
        mine = total[:, g * width : (g + 1) * width] + jnp.where(row == col, load, 0.0)
        acc[slot, :, g * width : (g + 1) * width] = jnp.where((row >= PANEL) & (col >= PANEL), mine, 0.0)
    for copy in out_copies(slot, step):
        copy.start()

    @pl.when(step == steps - 1)
    def _():
        for k in range(2):
            pltpu.make_async_copy(acc.at[k], acc.at[k], out_sem.at[k]).wait()


def trailing_part(spot, source, gather, rows, high, low, head, inv, load, so_far, snap, geo):
    tile, groups, width, stride, first, size = geo
    n, depth = rows.shape
    panel = head.shape[0]
    count = groups * width
    given = [spot, source, rows, high, low, head, inv, load]
    specs = [SMEM, ANY,
        vmem((tile, depth), lambda i: (i, 0)),
        vmem((tile, panel), lambda i: (i, 0)),
        vmem((tile, panel), lambda i: (i, 0)),
        vmem((panel, depth), lambda i: (0, 0)),
        vmem((panel, panel), lambda i: (0, 0)),
        vmem((1, size), lambda i: (0, 0)),
    ]
    alias = {}
    if so_far is not None:
        alias = {len(given): 0}
        given.append(so_far)
        specs.append(ANY)
    return pl.pallas_call(
        functools.partial(trailing_kernel, snap, geo, gather),
        grid=(n // tile,),
        out_shape=jax.ShapeDtypeStruct((n, size), F32),
        in_specs=specs,
        out_specs=ANY,
        scratch_shapes=[
            pltpu.VMEM((count, depth), BF16),
            pltpu.VMEM((count, panel), BF16),
            pltpu.VMEM((count, panel), BF16),
            pltpu.VMEM((2, tile, count), F32),
            pltpu.SemaphoreType.DMA((2,)),
            pltpu.SemaphoreType.DMA((groups,)),
        ],
        input_output_aliases=alias,
        compiler_params=pltpu.CompilerParams(vmem_limit_bytes=56 << 20),
        cost_estimate=cost(2 * n * count * (depth + 3 * panel), 2 * n * depth + 4 * n * count),
    )(*given)


def line_kernel(spot_ref, own, *refs):
    ups, downs, out, held, in_sem, out_sem = refs[:3], refs[3:6], refs[6], refs[7], refs[8], refs[9]
    n = own.shape[0]
    at = spot_ref[0]

    def pull(src, k):
        pltpu.make_async_copy(src, held.at[k], in_sem.at[k]).start()

    pull(own, 0)
    for j in range(1, 4):

        @pl.when(at >= j)
        def _(j=j):
            pull(ups[j - 1], j)

        @pl.when(at < j)
        def _(j=j):
            pull(downs[3 - j], j)

    pushes = []
    for j in range(4):
        pltpu.make_async_copy(held.at[j], held.at[j], in_sem.at[j]).wait()
        plane = jnp.where(at >= j, at - j, at - j + 4)
        push = pltpu.make_async_copy(held.at[j], out.at[pl.ds(pl.multiple_of(plane * n, n), n)], out_sem.at[j])
        push.start()
        pushes.append(push)
    for push in pushes:
        push.wait()


def in_line(spot, own, ups, downs):
    n, depth = own.shape
    return pl.pallas_call(
        line_kernel,
        out_shape=jax.ShapeDtypeStruct((4 * n, depth), own.dtype),
        in_specs=[SMEM] + [ANY] * 7,
        out_specs=ANY,
        scratch_shapes=[
            pltpu.VMEM((4, n, depth), own.dtype),
            pltpu.SemaphoreType.DMA((4,)),
            pltpu.SemaphoreType.DMA((4,)),
        ],
        compiler_params=pltpu.CompilerParams(vmem_limit_bytes=24 << 20),
        cost_estimate=cost(0, 16 * n * depth),
    )(spot, own, *ups, *downs)


def steer_of(delays, bin_index):
    angle = (delays * bin_index % NFFT).astype(F32) * (two_pi / NFFT)
    return jnp.concatenate([jnp.cos(angle), jnp.sin(angle)], axis=1)


def after(value, *others):
    return lax.optimization_barrier((value, *others))[0]


def planned(count):
    def move(value, pairs):
        return lax.ppermute(value, ("row", "col"), [(a * count + b, c * count + d) for (a, b), (c, d) in pairs])

    def across(m):
        return [((r, p), (r, p ^ m)) for r in range(count) for p in range(count)]

    def along(k, way):
        planes = [r for r in range(count) if 0 <= r + way < count and 0 <= r - way * (k - 1) < count]
        return [((r, p), (r + way, p)) for r in planes for p in range(count)]

    def hop(value, k):
        return [move(value[0], along(k, 1)), move(value[1], along(k, -1))]

    def chosen(index, values):
        out = values[-1]
        for k in range(len(values) - 2, -1, -1):
            out = jnp.where(index == k, values[k], out)
        return out

    def on_device(spectra, loading, delays, bin_index):
        row, col = lax.axis_index("row"), lax.axis_index("col")
        block, depth = spectra.shape
        size = delays.shape[0]
        snap = depth // 2
        early = block * 3 // 5
        spot_row = row.astype(jnp.int32).reshape(1)
        spot = jnp.stack([row, col]).astype(jnp.int32)

        quarter = PANEL // count
        quarters = [lax.slice_in_dim(spectra, j * quarter, (j + 1) * quarter) for j in range(count)]
        first = spectra[:early]
        head_load = loading[:PANEL].reshape(1, PANEL)

        own_rows = lax.all_gather(spectra, "col", axis=0, tiled=True)
        one = hop([first, first], 1)
        held = chosen(col, [quarters[0]] + [move(quarters[j], [((0, 0), (0, j))]) for j in range(1, count)])
        rest = lax.all_to_all(after(spectra[early:], held), "row", 0, 0, tiled=True)

        two = hop(one, 2)
        top = after(delays[:PANEL].astype(jnp.int16), *one)
        tops = [top] + [move(top, [((0, p), (k, p)) for p in range(count)]) for k in range(1, count)]
        held = after(held, *two, *tops, rest)
        rest = lax.all_to_all(rest, "col", 0, 0, tiled=True)

        lifted = [held] + [move(held, [((0, p), (k, p)) for p in range(count)]) for k in range(1, count)]
        three = hop([after(v, held) for v in two], 3)
        piece = after(chosen(row, lifted), rest, *tops, *three)

        stacked = in_line(spot_row, first, [one[0], two[0], three[0]], [one[1], two[1], three[1]])
        cols_first = lax.all_to_all(stacked, "col", 0, 0, tiled=True)
        cols_rest = lax.all_gather(rest, "row", axis=0, tiled=True)
        pieces = [piece] + [move(piece, across(m)) for m in range(1, count)]

        pieces = [after(v, stacked) for v in pieces]
        inv, head = head_factor(col.astype(jnp.int32).reshape(1), pieces, head_load, snap)
        steer_top = steer_of(chosen(row, tops).astype(jnp.int32), bin_index[0])
        steer = steer_of(delays, bin_index[0])
        panel, high, low, whitened = own_panel(
            spot_row, own_rows, head, inv, head_load, steer, steer_top, snap, PANEL
        )

        load = lax.dynamic_slice_in_dim(loading, col * size, size).reshape(1, size)
        tile = size // 8
        trailing = trailing_part(
            spot, cols_first, False, own_rows, high, low, head, inv, load, None, snap,
            (tile, count, early, block, 0, size),
        )
        trailing = trailing_part(
            spot, cols_rest, True, own_rows, high, low, head, inv, load, trailing, snap,
            (tile, count, block - early, block, early, size),
        )
        return (trailing, panel, whitened)

    return on_device


def from_root(value, axis, source):
    kept = jnp.where(lax.axis_index(axis) == source, value, 0).astype(value.dtype)
    return lax.psum(kept, axis)


def lower_solve(factor, right_side):
    return jax.scipy.linalg.solve_triangular(factor, right_side, lower=True)


def general(spectra, loading, delays, bin_index):
    row_index, col_index = lax.axis_index("row"), lax.axis_index("col")
    size, slow_count = delays.shape
    snap = spectra.shape[1] // 2
    own_rows = lax.all_gather(spectra, "col", axis=0, tiled=True)
    col_rows = from_root(own_rows, "row", col_index)
    row_load = lax.dynamic_slice_in_dim(loading, row_index * size, size)
    tile_csd = jnp.dot(own_rows, col_rows.T, preferred_element_type=F32) / snap
    tile_csd = tile_csd + jnp.where(row_index == col_index, jnp.diag(row_load), 0.0)
    head_rows = from_root(own_rows[:PANEL], "row", 0)
    head_csd = jnp.dot(head_rows, head_rows.T, preferred_element_type=F32) / snap
    factor = jnp.linalg.cholesky(head_csd + jnp.diag(loading[:PANEL]))
    head_load = jnp.eye(size, PANEL, dtype=F32) * loading[:PANEL][None, :]
    own_side = jnp.dot(own_rows, head_rows.T, preferred_element_type=F32) / snap
    own_side = own_side + jnp.where(row_index == 0, head_load, 0.0)
    col_side = jnp.dot(col_rows, head_rows.T, preferred_element_type=F32) / snap
    col_side = col_side + jnp.where(col_index == 0, head_load, 0.0)
    panel = lower_solve(factor, own_side.T).T
    col_panel = lower_solve(factor, col_side.T).T
    glob_rows = row_index * size + jnp.arange(size)
    glob_cols = col_index * size + jnp.arange(size)
    update = tile_csd - jnp.dot(panel, col_panel.T, precision=HIGHEST, preferred_element_type=F32)
    trailing = jnp.where((glob_rows[:, None] >= PANEL) & (glob_cols[None, :] >= PANEL), update, 0.0)
    steer = steer_of(delays, bin_index[0])
    solved = from_root(lower_solve(factor, steer[:PANEL]), "row", 0)
    lower_rows = steer - jnp.dot(panel, solved, precision=HIGHEST, preferred_element_type=F32)
    padded = jnp.pad(solved, ((0, size - PANEL), (0, 0)))
    stacked = jnp.where(glob_rows[:, None] < PANEL, padded, lower_rows)
    whitened = jnp.stack([stacked[:, :slow_count], stacked[:, slow_count:]])
    return (trailing, panel, whitened)


def solution(mesh):
    count = mesh.shape["col"]
    square = mesh.shape["row"] == count
    return jax.shard_map(
        planned(count) if square and count == 4 else general,
        mesh=mesh,
        in_specs=(P(("row", "col"), "freq"), P("freq"), P("row", "col"), P("freq")),
        out_specs=(
            P(("freq", "row"), "col"),
            P(("freq", "row"), None),
            P(None, ("freq", "row"), "col"),
        ),
        check_vma=False,
    )
```
